32 devices in a mesh: groups: 2 (over x), rows: 8 (over z, y), sub: 2 (over core).
Axes of the slice: x: 2, y: 2, z: 4, core: 2. Of those that a mesh axis runs over, the one named last changes fastest.
Arguments:
- database: bfloat16 [49152, 1536], P(('groups', 'rows', 'sub')), parts along dimension 0, may hold values from -6 to 6
- queries: bfloat16 [256, 1536], P(('groups', 'rows', 'sub')), parts along dimension 0, may hold values from -0.15625 to 0.15625
- probes: int32 [256, 12], P('groups'), parts along dimension 0, may hold values from 0 to 47, all different within a row
- block_list: int32 [384, 1], P(('groups', 'rows', 'sub')), parts along dimension 0, may hold values from 0 to 47
- neighbors: int32 [384, 8], P(('groups', 'rows', 'sub')), parts along dimension 0, may hold values from 0 to 191, as said below
- affinity: float32 [384, 8, 128, 128], P(('groups', 'rows', 'sub')), parts along dimension 0, may hold values from 0 to 10, as said below
Outputs:
- diffused: float32 [49152, 128], P(('groups', 'rows', 'sub')), parts along dimension 0
The draws below stay inside these ranges and needn't reach their ends.
There are 2 independent parts, one for each index of `groups`. The reference program is written for one: setup_inputs(seed, part) draws one part's arguments, and reference() takes and returns one part's arrays. A program takes and returns all parts, laid end to end along the dimension named above; each array names one. Nothing has to cross between parts.
Inputs may be any that keep to these rules, and one draw needn't show every extreme that they name: Column 0 names the block itself. For every other column j the blocks are paired two by two: neighbors[b, j] = c exactly when neighbors[c, j] = b, with c != b, and c lies among the blocks of the same device or among the nearer 12 // 2 blocks of an adjacent device along the row blocks. Entries are positive. The matrix W is symmetric: affinity[neighbors[b, j], j] is the transpose of affinity[b, j], and affinity[b, 0] is symmetric.
All inputs are finite; a program needn't handle non-finite values.
Results may differ from the reference program's by a relative error of at most 0.0003.
Values may be sent and summed in bfloat16 or wider, within the bound.
A program may use at most 64 MiB of HBM per device.

```python
import math
import jax
import jax.numpy as jnp
from jax import lax

D = 1536
QUERIES = 128
BLK = 128
K_BLK = 8
ITERS = 3
NBLK = 12
ROWS = 24576
NBLOCKS = 192
LISTS = 48
NPROBE = 12


def pairings(key):
    index_all = jnp.arange(NBLOCKS, dtype=jnp.int32)
    half_blocks = NBLK // 2
    columns_list = [index_all]
    for column in range(1, K_BLK):
        column_key = jax.random.fold_in(key, 100 + column)
        if column < K_BLK // 2:
            window_of = index_all // NBLK
        else:
            window_of = (index_all + half_blocks) // NBLK
        ranks = jax.random.permutation(column_key, NBLOCKS).astype(jnp.int32)
        ordering = jnp.argsort(window_of * NBLOCKS + ranks, stable=True).astype(jnp.int32)
        evens = ordering[0::2]
        odds = ordering[1::2]
        partner = jnp.zeros((NBLOCKS,), dtype=jnp.int32).at[evens].set(odds).at[odds].set(evens)
        columns_list.append(partner)
    return jnp.stack(columns_list, axis=1).astype(jnp.int32)


def draw_neighbors(key, part):
    return pairings(key)


def draw_affinity(key, part):
    table = pairings(key)
    key = jax.random.fold_in(key, 11)
    power = 2.0
    level_top = 3.0
    index_all = jnp.arange(NBLOCKS, dtype=jnp.int32)
    slabs = []
    for column in range(K_BLK):
        column_key = jax.random.fold_in(key, column)
        lower_ids = jnp.minimum(index_all, table[:, column])
        flipped = table[:, column] < index_all

        def one_block(lower_id, flip):
            block_key = jax.random.fold_in(column_key, lower_id)
            base = jax.random.uniform(block_key, (BLK, BLK), dtype=jnp.float32)
            level = jnp.exp(jax.random.uniform(jax.random.fold_in(block_key, 7), (), dtype=jnp.float32, minval=math.log(0.3), maxval=math.log(level_top)))
            values = base ** power * level
            if column == 0:
                values = 0.5 * (values + values.T)
            return jnp.where(flip, values.T, values)
        slabs.append(jax.vmap(one_block)(lower_ids, flipped))
    return jnp.stack(slabs, axis=1).astype(jnp.float32)


def block_levels(own_key, dims, split, low, high):
    def one(position, parts):
        draws = jax.random.uniform(jax.random.fold_in(jax.random.fold_in(own_key, 6), position), (parts,), jnp.float32, low / len(split), high / len(split))
        return jnp.repeat(jnp.exp(draws), dims[position] // parts).reshape((-1,) + (1,) * (len(dims) - position - 1))

    gain = one(*split[0])
    for cut in split[1:]:
        gain = gain * one(*cut)
    return gain


def picks_of(own_key, rows, count, top, lift):
    ranking = jax.random.permutation(jax.random.fold_in(own_key, 1), count)
    boost = ranking
    for power in range(3):
        boost = boost * boost // count
    boost = boost * lift // count
    chance = jax.random.randint(jax.random.fold_in(own_key, 2), (rows, count), 0, 4096) + boost
    fixed_rows = jax.random.permutation(jax.random.fold_in(own_key, 3), rows)[jnp.arange(count) % rows]
    chance = jnp.where(jnp.arange(rows)[:, None] == fixed_rows[None, :], 1 << 14, chance)
    merit = chance * count + jnp.arange(count)
    return lax.top_k(merit.astype(jnp.int32), top)[1].astype(jnp.int32)


def centred(own_key, dims, spread, most, split=(), kind=jnp.bfloat16):
    entries = spread * jax.random.normal(own_key, dims, jnp.float32)
    if split:
        entries = entries * block_levels(own_key, dims, split, -0.22, 0.18)
    return jnp.clip(entries, -most, most).astype(kind)


def setup_inputs(seed: int = 0, part: int = 0) -> dict:
    streams_of = jax.random.split(jax.random.key(seed), 7)
    part_keys = jax.random.split(jax.random.fold_in(streams_of[6], part), 7)
    database = centred(part_keys[0], (ROWS, D), 1.0, 6.0, ((0, 16),))
    queries = centred(part_keys[1], (QUERIES, D), D ** -0.5, 0.15625, ((0, 16),))
    probes = picks_of(part_keys[2], QUERIES, LISTS, NPROBE, 0)
    block_list = picks_of(part_keys[3], NBLOCKS, LISTS, 1, 0)
    neighbors = draw_neighbors(jax.random.fold_in(jax.random.fold_in(streams_of[6], part), 71), part)
    affinity = draw_affinity(jax.random.fold_in(jax.random.fold_in(streams_of[6], part), 71), part)
    return dict(database=database, queries=queries, probes=probes, block_list=block_list, neighbors=neighbors, affinity=affinity)


damping = 0.99

def reference(database, queries, probes, block_list, neighbors, affinity):
    block_total = affinity.shape[0]
    block_rows = affinity.shape[2]
    query_count = queries.shape[0]
    scores = jnp.dot(database, queries.T, preferred_element_type=jnp.float32)
    probed = jnp.any(block_list[:, 0][:, None, None] == probes[None, :, :], axis=2)
    grown = jnp.exp(scores).reshape(block_total, block_rows, query_count)
    seed_rows = jnp.where(probed[:, None, :], grown, jnp.zeros_like(grown)).reshape(-1, query_count)
    degree = lax.optimization_barrier(jnp.sum(affinity, axis=(1, 3))).reshape(-1, 1)
    inv_root = 1.0 / jnp.sqrt(degree)

    def operate(direction):
        scaled = (inv_root * direction).reshape(block_total, block_rows, query_count)
        product = jnp.zeros((block_total, block_rows, query_count), dtype=jnp.float32)
        for column in range(affinity.shape[1]):
            picked = scaled[neighbors[:, column]]
            product = product + jnp.einsum('irs,isq->irq', affinity[:, column], picked, precision=lax.Precision.HIGHEST)
        return direction - damping * inv_root * product.reshape(direction.shape)
    diffused = jnp.zeros_like(seed_rows)
    residual = seed_rows
    direction = seed_rows
    norm_now = lax.optimization_barrier(jnp.sum(residual * residual, axis=0))
    for turn_index in range(ITERS):
        image = operate(direction)
        step_size = norm_now / lax.optimization_barrier(jnp.sum(direction * image, axis=0))
        diffused = diffused + step_size * direction
        residual = residual - step_size * image
        norm_next = lax.optimization_barrier(jnp.sum(residual * residual, axis=0))
        direction = residual + norm_next / norm_now * direction
        norm_now = norm_next
    return diffused
```

```python
import functools

import jax
import jax.numpy as jnp
from jax import lax
from jax.experimental import pallas as pl
from jax.experimental.pallas import tpu as pltpu
from jax.sharding import PartitionSpec as P

ITERS = 3
damping = 0.99
PARTS = 2
MESH = pl.DeviceIdType.MESH
f32, bf16 = jnp.float32, jnp.bfloat16


def kernel(
    n, sub, pad, own, split,
    nb_ref, bl_ref, probes_ref, q_ref, db_hbm, aff_hbm,
    out_ref,
    gathered, query, db, aff, wcat, root,
    v0, v1, v2, v3, base, wide0, res1, wide1, dir1, res2,
    red0, red1, red2,
    aff_sem, db_sem, own_sem, q_send, q_recv, halo_send, halo_recv, red_send, red_recv,
):
    nblk, cols, blk, _ = aff.shape
    half = nblk // 2
    queries = out_ref.shape[1]
    me = lax.axis_index("rows") * sub + lax.axis_index("sub")

    def place(index):
        return {"rows": index // sub, "sub": lax.rem(index, sub)}

    def aff_copy(b):
        return pltpu.make_async_copy(aff_hbm.at[b], aff.at[b], aff_sem.at[b])

    chunks = db_sem.shape[0]
    chunk = db.shape[0] // chunks

    def db_copy(i):
        rows = pl.ds(i * chunk, chunk)
        return pltpu.make_async_copy(db_hbm.at[rows], db.at[rows], db_sem.at[i])

    own_copy = pltpu.make_async_copy(q_ref, gathered.at[me], own_sem)
    own_copy.start()
    for b in range(nblk):
        aff_copy(b).start()
    for i in range(chunks):
        db_copy(i).start()

    for v in (v0, v1, v2, v3):
        v[:, :half] = jnp.zeros((2, half, blk, queries), bf16)
        v[:, half + nblk:] = jnp.zeros((2, half, blk, queries), bf16)

    barrier = pltpu.get_barrier_semaphore()

    @pl.loop(1, n)
    def _(i):
        pl.semaphore_signal(barrier, inc=1, device_id=place(lax.rem(me + i, n)), device_id_type=MESH)

    pl.semaphore_wait(barrier, n - 1)

    def q_copy(peer):
        return pltpu.make_async_remote_copy(
            src_ref=q_ref, dst_ref=gathered.at[me], send_sem=q_send.at[peer], recv_sem=q_recv.at[me],
            device_id=place(peer), device_id_type=MESH,
        )

    def q_arrival(peer):
        return pltpu.make_async_remote_copy(
            src_ref=q_ref, dst_ref=gathered.at[peer], send_sem=q_send.at[peer], recv_sem=q_recv.at[peer],
            device_id=place(peer), device_id_type=MESH,
        )

    @pl.loop(1, n)
    def _(i):
        q_copy(lax.rem(me + i, n)).start()

    @pl.loop(0, nblk)
    def _(b):
        aff_copy(b).wait()
        total = jnp.zeros((blk, blk), f32)
        for j in range(cols):
            w = aff[b, j]
            total = total + w
            hi = w.astype(bf16)
            wcat[b, :blk, j * blk:(j + 1) * blk] = hi
            wcat[b, blk:, j * blk:(j + 1) * blk] = (w - hi.astype(f32)).astype(bf16)
        degree = jnp.sum(total, axis=1, keepdims=True)
        root[b] = jnp.broadcast_to(1.0 / jnp.sqrt(degree), (blk, queries))

    def put(v, index, u):
        hi = u.astype(bf16)
        v[0, index] = hi
        v[1, index] = (u - hi.astype(f32)).astype(bf16)

    def halo_copy(v, k, down):
        start, land = (half, half + nblk) if down else (nblk, 0)
        side = 2 * k + down
        peer = jnp.maximum(me - 1, 0) if down else jnp.minimum(me + 1, n - 1)
        return pltpu.make_async_remote_copy(
            src_ref=v.at[pl.ds(0, PARTS), pl.ds(start, half)],
            dst_ref=v.at[pl.ds(0, PARTS), pl.ds(land, half)],
            send_sem=halo_send.at[side], recv_sem=halo_recv.at[side],
            device_id=place(peer), device_id_type=MESH,
        )

    def halo_start(v, k, both=True):
        @pl.when(me > 0)
        def _():
            halo_copy(v, k, 1).start()
        if both:
            @pl.when(me < n - 1)
            def _():
                halo_copy(v, k, 0).start()

    def halo_wait(v, k, both=True):
        @pl.when(me < n - 1)
        def _():
            halo_copy(v, k, 1).wait_recv()
        if both:
            @pl.when(me > 0)
            def _():
                halo_copy(v, k, 0).wait_recv()

    def halo_sent(v, k, both=True):
        @pl.when(me > 0)
        def _():
            halo_copy(v, k, 1).wait_send()
        if both:
            @pl.when(me < n - 1)
            def _():
                halo_copy(v, k, 0).wait_send()

    def red_copy(red, k, peer, slot):
        return pltpu.make_async_remote_copy(
            src_ref=red.at[me], dst_ref=red.at[slot], send_sem=red_send.at[k, peer], recv_sem=red_recv.at[k, slot],
            device_id=place(peer), device_id_type=MESH,
        )

    def reduce_start(red, k, first, second):
        red[me] = jnp.concatenate([first, second], axis=0)

        @pl.loop(1, n)
        def _(i):
            peer = lax.rem(me + i, n)
            red_copy(red, k, peer, me).start()

    def reduce_wait(red, k):
        @pl.loop(1, n)
        def _(i):
            peer = lax.rem(me + i, n)
            red_copy(red, k, peer, peer).wait_recv()

        total = jnp.sum(red[...], axis=0)
        return (
            jnp.sum(total[:8], axis=0, keepdims=True),
            jnp.sum(total[8:], axis=0, keepdims=True),
        )

    def fold(values):
        return jnp.sum(values.reshape(blk // 8, 8, queries), axis=0)

    def weighed(v, b):
        picks = []
        for j in range(cols):
            slot = jnp.clip(nb_ref[b, j] - me * nblk + half, 0, 2 * nblk - 1)
            picks.append(jnp.concatenate([v[0, slot], v[1, slot]], axis=1))
        product = jnp.dot(wcat[b], jnp.concatenate(picks, axis=0), preferred_element_type=f32)
        return (product[:blk, :queries] + product[blk:, :queries]) + (product[:blk, queries:] + product[blk:, queries:])

    zero = jnp.zeros((8, queries), f32)

    own_copy.wait()

    @pl.loop(1, n)
    def _(i):
        q_arrival(lax.rem(me + i, n)).wait_recv()

    width = gathered.shape[2]
    flat = gathered[...].reshape(n * pad, width)
    row = lax.broadcasted_iota(jnp.int32, (queries, n * pad), 0)
    col = lax.broadcasted_iota(jnp.int32, (queries, n * pad), 1)
    for part in range(split):
        wanted = (row // own) * pad + part * own + row % own
        chosen = jnp.where(col == wanted, 1.0, 0.0).astype(bf16)
        query[:, part * width:(part + 1) * width] = jnp.dot(chosen, flat, preferred_element_type=f32).astype(bf16)

    per = nblk // chunks
    for i in range(chunks):
        db_copy(i).wait()

    @pl.loop(0, chunks, init_carry=zero)
    def norm0(i, carry):
        scores = lax.dot_general(
            db[pl.ds(i * chunk, chunk), :], query[...], (((1,), (1,)), ((), ())), preferred_element_type=f32
        )
        for t in range(per):
            b = i * per + t
            probed = jnp.max(jnp.where(probes_ref[...] == bl_ref[b, 0], 1.0, 0.0), axis=0, keepdims=True)
            seed = jnp.where(probed > 0.5, jnp.exp(scores[t * blk:(t + 1) * blk]), 0.0)
            base[b] = seed
            put(v0, half + b, root[b] * seed)
            carry = carry + fold(seed * seed)
        return carry

    halo_start(v0, 0)
    halo_wait(v0, 0)

    @pl.loop(0, nblk, init_carry=zero)
    def curve0(b, carry):
        seed = base[b]
        image = seed - damping * root[b] * weighed(v0, b)
        wide0[b] = image
        put(v1, half + b, root[b] * image)
        return carry + fold(seed * image)

    halo_start(v1, 1)
    reduce_start(red0, 0, norm0, curve0)
    gamma0, delta0 = reduce_wait(red0, 0)
    alpha0 = gamma0 / delta0
    halo_wait(v1, 1)

    @pl.loop(0, nblk, init_carry=(zero, zero))
    def dots1(b, carry):
        image = wide0[b]
        second = image - damping * root[b] * weighed(v1, b)
        residual = base[b] - alpha0 * image
        wide = image - alpha0 * second
        res1[b] = residual
        wide1[b] = wide
        put(v2, half + b, root[b] * wide)
        return carry[0] + fold(residual * residual), carry[1] + fold(residual * wide)

    halo_start(v2, 2, both=False)
    reduce_start(red1, 1, *dots1)
    gamma1, delta1 = reduce_wait(red1, 1)
    beta0 = gamma1 / gamma0
    alpha1 = gamma1 / (delta1 - beta0 * gamma1 / alpha0)

    @pl.loop(0, nblk, init_carry=zero)
    def norm2(b, carry):
        residual = res1[b] - alpha1 * (wide1[b] + beta0 * wide0[b])
        res2[b] = residual
        dir1[b] = res1[b] + beta0 * base[b]
        put(v3, half + b, root[b] * residual)
        return carry + fold(residual * residual)

    halo_wait(v2, 2, both=False)

    @pl.loop(half + nblk, 2 * nblk)
    def _(c):
        def value(v):
            return v[0, c].astype(f32) + v[1, c].astype(f32)
        first = value(v1)
        u = (value(v0) - alpha0 * first) - alpha1 * (value(v2) + beta0 * first)
        put(v3, c, 2.0 * u)

    @pl.loop(0, nblk, init_carry=zero)
    def cross2(b, carry):
        return carry + fold(res2[b] * root[b] * weighed(v3, b))

    reduce_start(red2, 2, norm2, norm2 - damping * cross2)
    gamma2, delta2 = reduce_wait(red2, 2)
    beta1 = gamma2 / gamma1
    alpha2 = gamma2 / (delta2 - beta1 * gamma2 / alpha1)
    gain = alpha1 + alpha2 * beta1

    @pl.loop(0, nblk)
    def _(b):
        out_ref[pl.ds(b * blk, blk), :] = alpha0 * base[b] + gain * dir1[b] + alpha2 * res2[b]

    halo_sent(v0, 0)
    halo_sent(v1, 1)
    halo_sent(v2, 2, both=False)

    @pl.loop(1, n)
    def _(i):
        peer = lax.rem(me + i, n)
        q_copy(peer).wait_send()
        red_copy(red0, 0, peer, me).wait_send()
        red_copy(red1, 1, peer, me).wait_send()
        red_copy(red2, 2, peer, me).wait_send()


def on_device(database, queries, probes, block_list, neighbors, affinity):
    nblk, cols, blk, _ = affinity.shape
    query_count = probes.shape[0]
    sub = lax.axis_size("sub")
    n = lax.axis_size("rows") * sub
    own, depth = queries.shape
    pad = 16
    split = max(1, pad // own) if own * 2 >= pad else 1
    pieces = queries.reshape(own, split, depth // split).transpose(1, 0, 2).reshape(own * split, depth // split)
    pad = -(-own * split // pad) * pad
    pieces = jnp.pad(pieces, ((0, pad - own * split), (0, 0)))
    vmem = pl.BlockSpec(memory_space=pltpu.VMEM)
    smem = pl.BlockSpec(memory_space=pltpu.SMEM)
    anywhere = pl.BlockSpec(memory_space=pl.ANY)
    blocks = pltpu.VMEM((nblk, blk, query_count), f32)
    zone = pltpu.VMEM((2, 2 * nblk, blk, query_count), bf16)
    sums = pltpu.VMEM((n, 16, query_count), f32)
    chunks = 4 if nblk % 4 == 0 else 1
    return pl.pallas_call(
        functools.partial(kernel, n, sub, pad, own, split),
        out_shape=jax.ShapeDtypeStruct((nblk * blk, query_count), f32),
        in_specs=[smem, smem, vmem, vmem, anywhere, anywhere],
        out_specs=vmem,
        scratch_shapes=[
            pltpu.VMEM((n, pad, depth // split), bf16),
            pltpu.VMEM((query_count, depth), bf16),
            pltpu.VMEM(database.shape, bf16),
            pltpu.VMEM(affinity.shape, f32),
            pltpu.VMEM((nblk, 2 * blk, cols * blk), bf16),
            blocks,
            zone, zone, zone, zone,
            blocks, blocks, blocks, blocks, blocks, blocks,
            sums, sums, sums,
            pltpu.SemaphoreType.DMA((nblk,)),
            pltpu.SemaphoreType.DMA((chunks,)),
            pltpu.SemaphoreType.DMA,
            pltpu.SemaphoreType.DMA((n,)),
            pltpu.SemaphoreType.DMA((n,)),
            pltpu.SemaphoreType.DMA((6,)),
            pltpu.SemaphoreType.DMA((6,)),
            pltpu.SemaphoreType.DMA((3, n)),
            pltpu.SemaphoreType.DMA((3, n)),
        ],
        compiler_params=pltpu.CompilerParams(
            collective_id=0, has_side_effects=True, vmem_limit_bytes=56 * 1024 * 1024
        ),
    )(neighbors, block_list, probes.T, pieces, database, affinity)


def solution(mesh):
    placed = (
        P(("groups", "rows", "sub"), None),
        P(("groups", "rows", "sub"), None),
        P("groups", None),
        P(("groups", "rows", "sub"), None),
        P(("groups", "rows", "sub"), None),
        P(("groups", "rows", "sub"), None, None, None),
    )
    return jax.shard_map(
        on_device,
        mesh=mesh,
        in_specs=placed,
        out_specs=P(("groups", "rows", "sub"), None),
        check_vma=False,
    )
```

```python
import functools

import jax
import jax.numpy as jnp
from jax import lax
from jax.experimental import pallas as pl
from jax.experimental.pallas import tpu as pltpu
from jax.sharding import PartitionSpec as P

ITERS = 3
damping = 0.99
UNROLL = 3
PARTS = (2, 2, 1)
MESH = pl.DeviceIdType.MESH
f32, bf16 = jnp.float32, jnp.bfloat16


def kernel(
    n, sub, pad, own, split,
    nb_hbm, bl_hbm, probes_ref, q_ref, db_hbm, aff_hbm,
    out_ref,
    nb_ref, bl_ref, gathered, query, db, aff, wcat, root,
    v0, v1, v2, base, wide0, wide1, wide2, res2,
    red0, red1, red2,
    small_sem, aff_sem, db_sem, own_sem, q_send, q_recv, pass_send, pass_recv, halo_send, halo_recv, red_send, red_recv,
):
    nblk, cols, blk, _ = aff.shape
    half = nblk // 2
    queries = out_ref.shape[1]
    me = lax.axis_index("rows") * sub + lax.axis_index("sub")

    def place(index):
        return {"rows": index // sub, "sub": lax.rem(index, sub)}

    def aff_copy(b):
        return pltpu.make_async_copy(aff_hbm.at[b], aff.at[b], aff_sem.at[b])

    chunks = db_sem.shape[0]
    chunk = db.shape[0] // chunks

    def db_copy(i):
        rows = pl.ds(i * chunk, chunk)
        return pltpu.make_async_copy(db_hbm.at[rows], db.at[rows], db_sem.at[i])

    nb_copy = pltpu.make_async_copy(nb_hbm, nb_ref, small_sem.at[0])
    bl_copy = pltpu.make_async_copy(bl_hbm, bl_ref, small_sem.at[1])
    nb_copy.start()
    bl_copy.start()
    own_copy = pltpu.make_async_copy(q_ref, gathered.at[me], own_sem)
    own_copy.start()
    for b in range(nblk):
        aff_copy(b).start()
    for i in range(chunks):
        db_copy(i).start()

    for v in (v0, v1, v2):
        v[:, :half] = jnp.zeros((2, half, blk, queries), bf16)
        v[:, half + nblk:] = jnp.zeros((2, half, blk, queries), bf16)

    barrier = pltpu.get_barrier_semaphore()

    @pl.loop(1, n)
    def _(i):
        pl.semaphore_signal(barrier, inc=1, device_id=place(lax.rem(me + i, n)), device_id_type=MESH)

    pl.semaphore_wait(barrier, n - 1)

    my_row, my_sub = me // sub, lax.rem(me, sub)
    rows = n // sub

    def q_copy(peer, slot):
        return pltpu.make_async_remote_copy(
            src_ref=q_ref, dst_ref=gathered.at[slot], send_sem=q_send.at[peer], recv_sem=q_recv.at[slot],
            device_id=place(peer), device_id_type=MESH,
        )

    def q_pass(slot, there, other):
        return pltpu.make_async_remote_copy(
            src_ref=gathered.at[slot], dst_ref=gathered.at[there],
            send_sem=pass_send.at[slot, other], recv_sem=pass_recv.at[there],
            device_id=place(my_row * sub + other), device_id_type=MESH,
        )

    @pl.loop(1, rows)
    def _(i):
        q_copy(lax.rem(my_row + i, rows) * sub + my_sub, me).start()

    own_copy.wait()
    for k in range(1, sub):
        q_pass(me, me, lax.rem(my_sub + k, sub)).start()

    @pl.loop(0, nblk)
    def _(b):
        aff_copy(b).wait()
        total = jnp.zeros((blk, blk), f32)
        for j in range(cols):
            w = aff[b, j]
            total = total + w
            hi = w.astype(bf16)
            wcat[b, :blk, j * blk:(j + 1) * blk] = hi
            wcat[b, blk:, j * blk:(j + 1) * blk] = (w - hi.astype(f32)).astype(bf16)
        degree = jnp.sum(total, axis=1, keepdims=True)
        root[b] = jnp.broadcast_to(1.0 / jnp.sqrt(degree), (blk, queries))

    def put(v, index, u):
        hi = u.astype(bf16)
        v[0, index] = hi
        v[1, index] = (u - hi.astype(f32)).astype(bf16)

    def halo_copy(v, k, down, i):
        start, land = (half, half + nblk) if down else (nblk, 0)
        peer = jnp.maximum(me - 1, 0) if down else jnp.minimum(me + 1, n - 1)
        return pltpu.make_async_remote_copy(
            src_ref=v.at[pl.ds(0, PARTS[k]), start + i],
            dst_ref=v.at[pl.ds(0, PARTS[k]), land + i],
            send_sem=halo_send.at[2 * k + down, i], recv_sem=halo_recv.at[2 * k + down, i],
            device_id=place(peer), device_id_type=MESH,
        )

    def halo_start(v, k, i):
        @pl.when(me > 0)
        def _():
            halo_copy(v, k, 1, i).start()
        @pl.when(me < n - 1)
        def _():
            halo_copy(v, k, 0, i).start()

    def halo_wait(v, k):
        @pl.when(me < n - 1)
        def _():
            @pl.loop(0, half)
            def _(i):
                halo_copy(v, k, 1, i).wait_recv()
        @pl.when(me > 0)
        def _():
            @pl.loop(0, half)
            def _(i):
                halo_copy(v, k, 0, i).wait_recv()

    def halo_sent(v, k):
        @pl.when(me > 0)
        def _():
            @pl.loop(0, half)
            def _(i):
                halo_copy(v, k, 1, i).wait_send()
        @pl.when(me < n - 1)
        def _():
            @pl.loop(0, half)
            def _(i):
                halo_copy(v, k, 0, i).wait_send()

    def red_copy(red, k, peer, slot):
        return pltpu.make_async_remote_copy(
            src_ref=red.at[me], dst_ref=red.at[slot], send_sem=red_send.at[k, peer], recv_sem=red_recv.at[k, slot],
            device_id=place(peer), device_id_type=MESH,
        )

    def reduce_start(red, k, first, second):
        red[me] = jnp.concatenate(
            [jnp.sum(first, axis=0, keepdims=True), jnp.sum(second, axis=0, keepdims=True)], axis=0
        )

        @pl.loop(1, n)
        def _(i):
            peer = lax.rem(me + i, n)
            red_copy(red, k, peer, me).start()

    def reduce_wait(red, k):
        @pl.loop(1, n)
        def _(i):
            peer = lax.rem(me + i, n)
            red_copy(red, k, peer, peer).wait_recv()

        total = jnp.sum(red[...], axis=0)
        return total[:1], total[1:]

    def fold(values):
        return jnp.sum(values.reshape(blk // 8, 8, queries), axis=0)

    def weighed(v, b):
        picks = []
        for j in range(cols):
            slot = jnp.clip(nb_ref[b, j] - me * nblk + half, 0, 2 * nblk - 1)
            picks.append(jnp.concatenate([v[0, slot], v[1, slot]], axis=1))
        product = jnp.dot(wcat[b], jnp.concatenate(picks, axis=0), preferred_element_type=f32)
        return (product[:blk, :queries] + product[blk:, :queries]) + (product[:blk, queries:] + product[blk:, queries:])

    zero = jnp.zeros((8, queries), f32)

    @pl.loop(1, rows)
    def _(i):
        slot = lax.rem(my_row + i, rows) * sub + my_sub
        q_copy(slot, slot).wait_recv()
        for k in range(1, sub):
            q_pass(slot, slot, lax.rem(my_sub + k, sub)).start()

    @pl.loop(0, rows)
    def _(i):
        row = lax.rem(my_row + i, rows)
        for k in range(1, sub):
            other = lax.rem(my_sub + k, sub)
            q_pass(row * sub + my_sub, row * sub + other, other).wait_recv()

    width = gathered.shape[2]
    flat = gathered[...].reshape(n * pad, width)
    row = lax.broadcasted_iota(jnp.int32, (queries, n * pad), 0)
    col = lax.broadcasted_iota(jnp.int32, (queries, n * pad), 1)
    for part in range(split):
        wanted = (row // own) * pad + part * own + row % own
        chosen = jnp.where(col == wanted, 1.0, 0.0).astype(bf16)
        query[:, part * width:(part + 1) * width] = jnp.dot(chosen, flat, preferred_element_type=f32).astype(bf16)

    for i in range(chunks):
        db_copy(i).wait()
    nb_copy.wait()
    bl_copy.wait()
    per = half // (chunks // 2)

    @pl.loop(0, chunks // 2, init_carry=zero)
    def norm0(i, carry):
        for side in range(2):
            first = side * half + i * per
            scores = lax.dot_general(
                db[pl.ds(first * blk, per * blk), :], query[...], (((1,), (1,)), ((), ())),
                preferred_element_type=f32,
            )
            for t in range(per):
                b = first + t
                probed = jnp.max(jnp.where(probes_ref[...] == bl_ref[b, 0], 1.0, 0.0), axis=0, keepdims=True)
                seed = jnp.where(probed > 0.5, jnp.exp(scores[t * blk:(t + 1) * blk]), 0.0)
                base[b] = seed
                put(v0, half + b, root[b] * seed)
                carry = carry + fold(seed * seed)
        for t in range(per):
            halo_start(v0, 0, i * per + t)
        return carry

    halo_wait(v0, 0)

    @pl.loop(0, half, init_carry=zero, unroll=UNROLL)
    def curve0(i, carry):
        for b in (i, half + i):
            seed = base[b]
            image = seed - damping * root[b] * weighed(v0, b)
            wide0[b] = image
            put(v1, half + b, root[b] * image)
            carry = carry + fold(seed * image)
        halo_start(v1, 1, i)
        return carry

    reduce_start(red0, 0, norm0, curve0)
    halo_wait(v1, 1)

    @pl.loop(0, half, unroll=UNROLL)
    def _(i):
        for b in (i, half + i):
            image = wide0[b] - damping * root[b] * weighed(v1, b)
            wide1[b] = image
            put(v2, half + b, root[b] * image)
        halo_start(v2, 2, i)

    gamma0, delta0 = reduce_wait(red0, 0)
    alpha0 = gamma0 / delta0

    def first_residual(b):
        return base[b] - alpha0 * wide0[b], wide0[b] - alpha0 * wide1[b]

    @pl.loop(0, nblk, init_carry=(zero, zero))
    def dots1(b, carry):
        residual, image = first_residual(b)
        return carry[0] + fold(residual * residual), carry[1] + fold(residual * image)

    reduce_start(red1, 1, *dots1)
    halo_wait(v2, 2)

    @pl.loop(0, half, unroll=UNROLL)
    def _(i):
        for b in (i, half + i):
            wide2[b] = wide1[b] - damping * root[b] * weighed(v2, b)

    gamma1, delta1 = reduce_wait(red1, 1)
    beta0 = gamma1 / gamma0
    alpha1 = gamma1 / (delta1 - beta0 * gamma1 / alpha0)

    @pl.loop(0, nblk, init_carry=(zero, zero))
    def dots2(b, carry):
        residual, image = first_residual(b)
        second = wide1[b] - alpha0 * wide2[b]
        later = residual - alpha1 * (image + beta0 * wide0[b])
        image = image - alpha1 * (second + beta0 * wide1[b])
        res2[b] = later
        return carry[0] + fold(later * later), carry[1] + fold(later * image)

    reduce_start(red2, 2, *dots2)
    gamma2, delta2 = reduce_wait(red2, 2)
    beta1 = gamma2 / gamma1
    alpha2 = gamma2 / (delta2 - beta1 * gamma2 / alpha1)
    gain = alpha1 + alpha2 * beta1
    on_base = alpha0 + gain * (1.0 + beta0)
    on_wide = gain * alpha0

    @pl.loop(0, nblk)
    def _(b):
        out_ref[pl.ds(b * blk, blk), :] = on_base * base[b] - on_wide * wide0[b] + alpha2 * res2[b]

    halo_sent(v0, 0)
    halo_sent(v1, 1)
    halo_sent(v2, 2)

    @pl.loop(1, n)
    def _(i):
        peer = lax.rem(me + i, n)
        red_copy(red0, 0, peer, me).wait_send()
        red_copy(red1, 1, peer, me).wait_send()
        red_copy(red2, 2, peer, me).wait_send()

    @pl.loop(1, rows)
    def _(i):
        q_copy(lax.rem(my_row + i, rows) * sub + my_sub, me).wait_send()

    @pl.loop(0, rows)
    def _(i):
        slot = lax.rem(my_row + i, rows) * sub + my_sub
        for k in range(1, sub):
            q_pass(slot, slot, lax.rem(my_sub + k, sub)).wait_send()


def on_device(database, queries, probes, block_list, neighbors, affinity):
    nblk, cols, blk, _ = affinity.shape
    query_count = probes.shape[0]
    sub = lax.axis_size("sub")
    n = lax.axis_size("rows") * sub
    own, depth = queries.shape
    pad = 16
    split = max(1, pad // own) if own * 2 >= pad else 1
    pieces = queries.reshape(own, split, depth // split).transpose(1, 0, 2).reshape(own * split, depth // split)
    pad = -(-own * split // pad) * pad
    pieces = jnp.pad(pieces, ((0, pad - own * split), (0, 0)))
    vmem = pl.BlockSpec(memory_space=pltpu.VMEM)
    anywhere = pl.BlockSpec(memory_space=pl.ANY)
    blocks = pltpu.VMEM((nblk, blk, query_count), f32)
    zone = pltpu.VMEM((2, 2 * nblk, blk, query_count), bf16)
    sums = pltpu.VMEM((n, 2, query_count), f32)
    chunks = 6 if nblk % 12 == 0 else 2
    return pl.pallas_call(
        functools.partial(kernel, n, sub, pad, own, split),
        out_shape=jax.ShapeDtypeStruct((nblk * blk, query_count), f32),
        in_specs=[anywhere, anywhere, vmem, vmem, anywhere, anywhere],
        out_specs=vmem,
        scratch_shapes=[
            pltpu.SMEM(neighbors.shape, jnp.int32),
            pltpu.SMEM(block_list.shape, jnp.int32),
            pltpu.VMEM((n, pad, depth // split), bf16),
            pltpu.VMEM((query_count, depth), bf16),
            pltpu.VMEM(database.shape, bf16),
            pltpu.VMEM(affinity.shape, f32),
            pltpu.VMEM((nblk, 2 * blk, cols * blk), bf16),
            blocks,
            zone, zone, zone,
            blocks, blocks, blocks, blocks, blocks,
            sums, sums, sums,
            pltpu.SemaphoreType.DMA((2,)),
            pltpu.SemaphoreType.DMA((nblk,)),
            pltpu.SemaphoreType.DMA((chunks,)),
            pltpu.SemaphoreType.DMA,
            pltpu.SemaphoreType.DMA((n,)),
            pltpu.SemaphoreType.DMA((n,)),
            pltpu.SemaphoreType.DMA((n, sub)),
            pltpu.SemaphoreType.DMA((n,)),
            pltpu.SemaphoreType.DMA((6, nblk // 2)),
            pltpu.SemaphoreType.DMA((6, nblk // 2)),
            pltpu.SemaphoreType.DMA((3, n)),
            pltpu.SemaphoreType.DMA((3, n)),
        ],
        compiler_params=pltpu.CompilerParams(
            collective_id=0, has_side_effects=True, vmem_limit_bytes=56 * 1024 * 1024
        ),
    )(neighbors, block_list, probes.T, pieces, database, affinity)


def solution(mesh):
    placed = (
        P(("groups", "rows", "sub"), None),
        P(("groups", "rows", "sub"), None),
        P("groups", None),
        P(("groups", "rows", "sub"), None),
        P(("groups", "rows", "sub"), None),
        P(("groups", "rows", "sub"), None, None, None),
    )
    return jax.shard_map(
        on_device,
        mesh=mesh,
        in_specs=placed,
        out_specs=P(("groups", "rows", "sub"), None),
        check_vma=False,
    )
```

```python
import functools

import jax
import jax.numpy as jnp
from jax import lax
from jax.experimental import pallas as pl
from jax.experimental.pallas import tpu as pltpu
from jax.sharding import PartitionSpec as P

ITERS = 3
damping = 0.99
UNROLL = 3
PARTS = (2, 1, 1)
MESH = pl.DeviceIdType.MESH
f32, bf16 = jnp.float32, jnp.bfloat16


def kernel(
    n, sub, pad, own, split,
    nb_hbm, bl_hbm, probes_ref, q_ref, db_hbm, aff_hbm,
    out_ref,
    nb_ref, bl_ref, gathered, query, db, aff, wcat, root,
    v0, v1, v2, t1, t2, base, wide0, wide1, wide2, res2,
    red0, red1, red2,
    small_sem, aff_sem, db_sem, own_sem, q_send, q_recv, pass_send, pass_recv, halo_send, halo_recv, red_send, red_recv,
):
    nblk, cols, blk, _ = aff.shape
    half = nblk // 2
    queries = out_ref.shape[1]
    me = lax.axis_index("rows") * sub + lax.axis_index("sub")

    def place(index):
        return {"rows": index // sub, "sub": lax.rem(index, sub)}

    def aff_copy(b):
        return pltpu.make_async_copy(aff_hbm.at[b], aff.at[b], aff_sem.at[b])

    chunks = db_sem.shape[0]
    chunk = db.shape[0] // chunks

    def db_copy(i):
        rows = pl.ds(i * chunk, chunk)
        return pltpu.make_async_copy(db_hbm.at[rows], db.at[rows], db_sem.at[i])

    nb_copy = pltpu.make_async_copy(nb_hbm, nb_ref, small_sem.at[0])
    bl_copy = pltpu.make_async_copy(bl_hbm, bl_ref, small_sem.at[1])
    nb_copy.start()
    bl_copy.start()
    own_copy = pltpu.make_async_copy(q_ref, gathered.at[me], own_sem)
    own_copy.start()
    for b in range(nblk):
        aff_copy(b).start()
    for i in range(chunks):
        db_copy(i).start()

    for v in (v0, t1, t2):
        v[:, :half] = jnp.zeros((v.shape[0], half, blk, queries), bf16)
        v[:, half + nblk:] = jnp.zeros((v.shape[0], half, blk, queries), bf16)

    barrier = pltpu.get_barrier_semaphore()

    @pl.loop(1, n)
    def _(i):
        pl.semaphore_signal(barrier, inc=1, device_id=place(lax.rem(me + i, n)), device_id_type=MESH)

    pl.semaphore_wait(barrier, n - 1)

    my_row, my_sub = me // sub, lax.rem(me, sub)
    rows = n // sub

    def q_copy(peer, slot):
        return pltpu.make_async_remote_copy(
            src_ref=q_ref, dst_ref=gathered.at[slot], send_sem=q_send.at[peer], recv_sem=q_recv.at[slot],
            device_id=place(peer), device_id_type=MESH,
        )

    def q_pass(slot, there, other):
        return pltpu.make_async_remote_copy(
            src_ref=gathered.at[slot], dst_ref=gathered.at[there],
            send_sem=pass_send.at[slot, other], recv_sem=pass_recv.at[there],
            device_id=place(my_row * sub + other), device_id_type=MESH,
        )

    @pl.loop(1, rows)
    def _(i):
        q_copy(lax.rem(my_row + i, rows) * sub + my_sub, me).start()

    own_copy.wait()
    for k in range(1, sub):
        q_pass(me, me, lax.rem(my_sub + k, sub)).start()

    @pl.loop(0, nblk)
    def _(b):
        aff_copy(b).wait()
        total = jnp.zeros((blk, blk), f32)
        for j in range(cols):
            w = aff[b, j]
            total = total + w
            hi = w.astype(bf16)
            wcat[b, :blk, j * blk:(j + 1) * blk] = hi
            wcat[b, blk:, j * blk:(j + 1) * blk] = (w - hi.astype(f32)).astype(bf16)
        degree = jnp.sum(total, axis=1, keepdims=True)
        root[b] = jnp.broadcast_to(1.0 / jnp.sqrt(degree), (blk, queries))

    def put(v, index, u):
        hi = u.astype(bf16)
        v[0, index] = hi
        v[1, index] = (u - hi.astype(f32)).astype(bf16)

    def halo_copy(v, k, down, i):
        start, land = (half, half + nblk) if down else (nblk, 0)
        peer = jnp.maximum(me - 1, 0) if down else jnp.minimum(me + 1, n - 1)
        return pltpu.make_async_remote_copy(
            src_ref=v.at[pl.ds(0, PARTS[k]), start + i],
            dst_ref=v.at[pl.ds(0, PARTS[k]), land + i],
            send_sem=halo_send.at[2 * k + down, i], recv_sem=halo_recv.at[2 * k + down, i],
            device_id=place(peer), device_id_type=MESH,
        )

    def halo_start(v, k, i):
        @pl.when(me > 0)
        def _():
            halo_copy(v, k, 1, i).start()
        @pl.when(me < n - 1)
        def _():
            halo_copy(v, k, 0, i).start()

    def halo_wait(v, k):
        @pl.when(me < n - 1)
        def _():
            @pl.loop(0, half)
            def _(i):
                halo_copy(v, k, 1, i).wait_recv()
        @pl.when(me > 0)
        def _():
            @pl.loop(0, half)
            def _(i):
                halo_copy(v, k, 0, i).wait_recv()

    def halo_sent(v, k):
        @pl.when(me > 0)
        def _():
            @pl.loop(0, half)
            def _(i):
                halo_copy(v, k, 1, i).wait_send()
        @pl.when(me < n - 1)
        def _():
            @pl.loop(0, half)
            def _(i):
                halo_copy(v, k, 0, i).wait_send()

    def red_copy(red, k, peer, slot):
        return pltpu.make_async_remote_copy(
            src_ref=red.at[me], dst_ref=red.at[slot], send_sem=red_send.at[k, peer], recv_sem=red_recv.at[k, slot],
            device_id=place(peer), device_id_type=MESH,
        )

    def reduce_start(red, k, first, second):
        red[me] = jnp.concatenate(
            [jnp.sum(first, axis=0, keepdims=True), jnp.sum(second, axis=0, keepdims=True)], axis=0
        )

        @pl.loop(1, n)
        def _(i):
            peer = lax.rem(me + i, n)
            red_copy(red, k, peer, me).start()

    def reduce_wait(red, k):
        @pl.loop(1, n)
        def _(i):
            peer = lax.rem(me + i, n)
            red_copy(red, k, peer, peer).wait_recv()

        total = jnp.sum(red[...], axis=0)
        return total[:1], total[1:]

    def fold(values):
        return jnp.sum(values.reshape(blk // 8, 8, queries), axis=0)

    def weighed(v, b):
        picks = []
        for j in range(cols):
            slot = jnp.clip(nb_ref[b, j] - me * nblk + half, 0, 2 * nblk - 1)
            picks.append(jnp.concatenate([v[0, slot], v[1, slot]], axis=1))
        product = jnp.dot(wcat[b], jnp.concatenate(picks, axis=0), preferred_element_type=f32)
        return (product[:blk, :queries] + product[blk:, :queries]) + (product[:blk, queries:] + product[blk:, queries:])

    def widen(v, before, change):
        for start in (0, half + nblk):
            @pl.loop(start, start + half)
            def _(c):
                known = before[0, c].astype(f32) + before[1, c].astype(f32)
                put(v, c, known - change[0, c].astype(f32))

    zero = jnp.zeros((8, queries), f32)

    @pl.loop(1, rows)
    def _(i):
        slot = lax.rem(my_row + i, rows) * sub + my_sub
        q_copy(slot, slot).wait_recv()
        for k in range(1, sub):
            q_pass(slot, slot, lax.rem(my_sub + k, sub)).start()

    @pl.loop(0, rows)
    def _(i):
        row = lax.rem(my_row + i, rows)
        for k in range(1, sub):
            other = lax.rem(my_sub + k, sub)
            q_pass(row * sub + my_sub, row * sub + other, other).wait_recv()

    width = gathered.shape[2]
    flat = gathered[...].reshape(n * pad, width)
    row = lax.broadcasted_iota(jnp.int32, (queries, n * pad), 0)
    col = lax.broadcasted_iota(jnp.int32, (queries, n * pad), 1)
    for part in range(split):
        wanted = (row // own) * pad + part * own + row % own
        chosen = jnp.where(col == wanted, 1.0, 0.0).astype(bf16)
        query[:, part * width:(part + 1) * width] = jnp.dot(chosen, flat, preferred_element_type=f32).astype(bf16)

    for i in range(chunks):
        db_copy(i).wait()
    nb_copy.wait()
    bl_copy.wait()
    per = half // (chunks // 2)

    @pl.loop(0, chunks // 2, init_carry=zero)
    def norm0(i, carry):
        for side in range(2):
            first = side * half + i * per
            scores = lax.dot_general(
                db[pl.ds(first * blk, per * blk), :], query[...], (((1,), (1,)), ((), ())),
                preferred_element_type=f32,
            )
            for t in range(per):
                b = first + t
                probed = jnp.max(jnp.where(probes_ref[...] == bl_ref[b, 0], 1.0, 0.0), axis=0, keepdims=True)
                seed = jnp.where(probed > 0.5, jnp.exp(scores[t * blk:(t + 1) * blk]), 0.0)
                base[b] = seed
                put(v0, half + b, root[b] * seed)
                carry = carry + fold(seed * seed)
        for t in range(per):
            halo_start(v0, 0, i * per + t)
        return carry

    halo_wait(v0, 0)

    @pl.loop(0, half, init_carry=zero, unroll=UNROLL)
    def curve0(i, carry):
        for b in (i, half + i):
            seed = base[b]
            drop = damping * root[b] * weighed(v0, b)
            image = seed - drop
            wide0[b] = image
            t1[0, half + b] = (root[b] * drop).astype(bf16)
            put(v1, half + b, root[b] * image)
            carry = carry + fold(seed * image)
        halo_start(t1, 1, i)
        return carry

    reduce_start(red0, 0, norm0, curve0)
    halo_wait(t1, 1)
    widen(v1, v0, t1)

    @pl.loop(0, half, unroll=UNROLL)
    def _(i):
        for b in (i, half + i):
            drop = damping * root[b] * weighed(v1, b)
            image = wide0[b] - drop
            wide1[b] = image
            t2[0, half + b] = (root[b] * drop).astype(bf16)
            put(v2, half + b, root[b] * image)
        halo_start(t2, 2, i)

    gamma0, delta0 = reduce_wait(red0, 0)
    alpha0 = gamma0 / delta0

    def first_residual(b):
        return base[b] - alpha0 * wide0[b], wide0[b] - alpha0 * wide1[b]

    @pl.loop(0, nblk, init_carry=(zero, zero))
    def dots1(b, carry):
        residual, image = first_residual(b)
        return carry[0] + fold(residual * residual), carry[1] + fold(residual * image)

    reduce_start(red1, 1, *dots1)
    halo_wait(t2, 2)
    widen(v2, v1, t2)

    @pl.loop(0, half, unroll=UNROLL)
    def _(i):
        for b in (i, half + i):
            wide2[b] = wide1[b] - damping * root[b] * weighed(v2, b)

    gamma1, delta1 = reduce_wait(red1, 1)
    beta0 = gamma1 / gamma0
    alpha1 = gamma1 / (delta1 - beta0 * gamma1 / alpha0)

    @pl.loop(0, nblk, init_carry=(zero, zero))
    def dots2(b, carry):
        residual, image = first_residual(b)
        second = wide1[b] - alpha0 * wide2[b]
        later = residual - alpha1 * (image + beta0 * wide0[b])
        image = image - alpha1 * (second + beta0 * wide1[b])
        res2[b] = later
        return carry[0] + fold(later * later), carry[1] + fold(later * image)

    reduce_start(red2, 2, *dots2)
    gamma2, delta2 = reduce_wait(red2, 2)
    beta1 = gamma2 / gamma1
    alpha2 = gamma2 / (delta2 - beta1 * gamma2 / alpha1)
    gain = alpha1 + alpha2 * beta1
    on_base = alpha0 + gain * (1.0 + beta0)
    on_wide = gain * alpha0

    @pl.loop(0, nblk)
    def _(b):
        out_ref[pl.ds(b * blk, blk), :] = on_base * base[b] - on_wide * wide0[b] + alpha2 * res2[b]

    halo_sent(v0, 0)
    halo_sent(t1, 1)
    halo_sent(t2, 2)

    @pl.loop(1, n)
    def _(i):
        peer = lax.rem(me + i, n)
        red_copy(red0, 0, peer, me).wait_send()
        red_copy(red1, 1, peer, me).wait_send()
        red_copy(red2, 2, peer, me).wait_send()

    @pl.loop(1, rows)
    def _(i):
        q_copy(lax.rem(my_row + i, rows) * sub + my_sub, me).wait_send()

    @pl.loop(0, rows)
    def _(i):
        slot = lax.rem(my_row + i, rows) * sub + my_sub
        for k in range(1, sub):
            q_pass(slot, slot, lax.rem(my_sub + k, sub)).wait_send()


def on_device(database, queries, probes, block_list, neighbors, affinity):
    nblk, cols, blk, _ = affinity.shape
    query_count = probes.shape[0]
    sub = lax.axis_size("sub")
    n = lax.axis_size("rows") * sub
    own, depth = queries.shape
    pad = 16
    split = max(1, pad // own) if own * 2 >= pad else 1
    pieces = queries.reshape(own, split, depth // split).transpose(1, 0, 2).reshape(own * split, depth // split)
    pad = -(-own * split // pad) * pad
    pieces = jnp.pad(pieces, ((0, pad - own * split), (0, 0)))
    vmem = pl.BlockSpec(memory_space=pltpu.VMEM)
    anywhere = pl.BlockSpec(memory_space=pl.ANY)
    blocks = pltpu.VMEM((nblk, blk, query_count), f32)
    change = pltpu.VMEM((1, 2 * nblk, blk, query_count), bf16)
    zone = pltpu.VMEM((2, 2 * nblk, blk, query_count), bf16)
    sums = pltpu.VMEM((n, 2, query_count), f32)
    chunks = 6 if nblk % 12 == 0 else 2
    return pl.pallas_call(
        functools.partial(kernel, n, sub, pad, own, split),
        out_shape=jax.ShapeDtypeStruct((nblk * blk, query_count), f32),
        in_specs=[anywhere, anywhere, vmem, vmem, anywhere, anywhere],
        out_specs=vmem,
        scratch_shapes=[
            pltpu.SMEM(neighbors.shape, jnp.int32),
            pltpu.SMEM(block_list.shape, jnp.int32),
            pltpu.VMEM((n, pad, depth // split), bf16),
            pltpu.VMEM((query_count, depth), bf16),
            pltpu.VMEM(database.shape, bf16),
            pltpu.VMEM(affinity.shape, f32),
            pltpu.VMEM((nblk, 2 * blk, cols * blk), bf16),
            blocks,
            zone, zone, zone, change, change,
            blocks, blocks, blocks, blocks, blocks,
            sums, sums, sums,
            pltpu.SemaphoreType.DMA((2,)),
            pltpu.SemaphoreType.DMA((nblk,)),
            pltpu.SemaphoreType.DMA((chunks,)),
            pltpu.SemaphoreType.DMA,
            pltpu.SemaphoreType.DMA((n,)),
            pltpu.SemaphoreType.DMA((n,)),
            pltpu.SemaphoreType.DMA((n, sub)),
            pltpu.SemaphoreType.DMA((n,)),
            pltpu.SemaphoreType.DMA((6, nblk // 2)),
            pltpu.SemaphoreType.DMA((6, nblk // 2)),
            pltpu.SemaphoreType.DMA((3, n)),
            pltpu.SemaphoreType.DMA((3, n)),
        ],
        compiler_params=pltpu.CompilerParams(
            collective_id=0, has_side_effects=True, vmem_limit_bytes=56 * 1024 * 1024
        ),
    )(neighbors, block_list, probes.T, pieces, database, affinity)


def solution(mesh):
    placed = (
        P(("groups", "rows", "sub"), None),
        P(("groups", "rows", "sub"), None),
        P("groups", None),
        P(("groups", "rows", "sub"), None),
        P(("groups", "rows", "sub"), None),
        P(("groups", "rows", "sub"), None, None, None),
    )
    return jax.shard_map(
        on_device,
        mesh=mesh,
        in_specs=placed,
        out_specs=P(("groups", "rows", "sub"), None),
        check_vma=False,
    )
```
